128 devices in a mesh: row: 16 (over y, z), col: 8 (over x, core).
Axes of the slice: x: 4, y: 4, z: 4, core: 2. Of those that a mesh axis runs over, the one named last changes fastest.
Arguments:
- load_vectors: bfloat16 [1024, 64, 384], P(('row', 'col')), may hold values from -6 to 6
- live_panels: int32 [1024], P(('row', 'col')), may hold values from 64 to 128
- self_blocks: bfloat16 [1024, 384, 384], P(('row', 'col')), may hold values from -0.3125 to 0.3125
- near_pairs: int32 [6144, 2], P(('row', 'col')), may hold values from 0 to 1023, as said below
- near_count: int32 [128], P(('row', 'col')), may hold values from 1 to 48, as said below
- near_blocks: bfloat16 [6144, 384, 384], P(('row', 'col')), may hold values from -0.3125 to 0.3125
- far_pairs: int32 [12288, 2], P(('row', 'col')), may hold values from 0 to 1023, as said below
- far_rank: int32 [12288], P(('row', 'col')), may hold values from 8 to 32, as said below
- far_left: bfloat16 [12288, 384, 32], P(('row', 'col')), may hold values from -1 to 1
- far_right: bfloat16 [12288, 384, 32], P(('row', 'col')), may hold values from -0.3125 to 0.3125
Outputs:
- product: float32 [1024, 64, 384], P(('row', 'col'))
The draws below stay inside these ranges and needn't reach their ends.
Inputs may be any that keep to these rules, and one draw needn't show every extreme that they name: `near_pairs`: slot s of group g = 8 a + b names a row cluster r with r // 64 = a and a column cluster c with (c // 8) mod 8 = b, and r != c. `far_pairs`: the same layout as near_pairs, with 96 slots a group. `near_count`: some group uses all of its slots. `far_rank`: some pair has the largest rank.
All inputs are finite; a program needn't handle non-finite values.
Results may differ from the reference program's by a relative error of at most 0.0065.
Values may be sent and summed in bfloat16 or wider, within the bound.
No kernel may reach another device: no remote copies, remote signals or barrier semaphores. Data moves between devices by JAX's collectives and lax.ppermute only.
A program may use at most 128 MiB of HBM per device.

```python
import jax
import jax.numpy as jnp
from jax import lax

PANELS = 128
DOF = 384
LOADS = 64
RANK = 32
CPD = 8
NP_DEV = 48
FP_DEV = 96
NCLUS = 1024
N_ROW = 16
N_COL = 8
DEVICES = 128


def pair_list(key, slots):
    groups = N_ROW * N_COL
    group_of = jnp.arange(groups * slots, dtype=jnp.int32) // slots
    block_row = group_of // N_COL
    block_col = group_of % N_COL
    key_one, key_two, key_three, key_four = jax.random.split(key, 4)
    total = groups * slots
    row_piece = block_row * N_COL + jax.random.randint(key_one, (total,), 0, N_COL)
    row_cluster = row_piece * CPD + jax.random.randint(key_two, (total,), 0, CPD)
    other_row = jax.random.randint(key_three, (total,), 0, N_ROW)
    col_piece = other_row * N_COL + block_col
    col_piece = jnp.where(col_piece == row_piece, (other_row + 1) % N_ROW * N_COL + block_col, col_piece)
    col_cluster = col_piece * CPD + jax.random.randint(key_four, (total,), 0, CPD)
    return jnp.stack([row_cluster, col_cluster], axis=1).astype(jnp.int32)


def draw_near_pairs(key, part):
    key = jax.random.fold_in(key, 11)
    return pair_list(key, NP_DEV)


def draw_far_pairs(key, part):
    key = jax.random.fold_in(key, 12)
    return pair_list(key, FP_DEV)


def draw_near_count(key, part):
    key = jax.random.fold_in(key, 13)
    key_one, key_two = jax.random.split(key)
    groups = N_ROW * N_COL
    draw_base = jax.random.randint(key_one, (groups,), 0, NP_DEV)
    counts = 1 + draw_base * draw_base // NP_DEV
    busiest = jax.random.randint(key_two, (), 0, groups)
    return jnp.where(jnp.arange(groups) == busiest, NP_DEV, counts).astype(jnp.int32)


def draw_far_rank(key, part):
    key = jax.random.fold_in(key, 14)
    key_one, key_two = jax.random.split(key)
    total = N_ROW * N_COL * FP_DEV
    ranks = jax.random.randint(key_one, (total,), RANK // 4, RANK + 1)
    widest = jax.random.randint(key_two, (), 0, total)
    return jnp.where(jnp.arange(total) == widest, RANK, ranks).astype(jnp.int32)


def plant(entries, key, least, largest):
    spot = [jax.random.randint(jax.random.fold_in(key, axis), (), 0, length) for axis, length in enumerate(entries.shape)]
    widest = entries.shape.index(max(entries.shape))
    neighbour = spot[:widest] + [(spot[widest] + 1) % entries.shape[widest]] + spot[widest + 1:]
    return entries.at[tuple(spot)].set(least).at[tuple(neighbour)].set(largest)


def steps_of(own_key, extent, cuts, least, top_value):
    gain, own = 1.0, jax.random.fold_in(own_key, 6)
    for dim, parts in cuts:
        heights = jnp.exp(jax.random.uniform(jax.random.fold_in(own, dim), (parts,), jnp.float32, least / len(cuts), top_value / len(cuts)))
        gain = gain * jnp.repeat(heights, extent[dim] // parts).reshape([-1 if axis == dim else 1 for axis in range(len(extent))])
    return gain


def gaussian(stream_key, dims, deviation, reach, cuts=(), held_as=jnp.bfloat16):
    drawn = deviation * jax.random.normal(stream_key, dims, jnp.float32)
    if cuts:
        drawn = drawn * steps_of(stream_key, dims, cuts, -0.22, 0.18)
    return jnp.clip(drawn, -reach, reach).astype(held_as)


def setup_inputs(seed: int = 0) -> dict:
    key_list = jax.random.split(jax.random.key(seed), 11)
    load_vectors = gaussian(key_list[0], (NCLUS, LOADS, DOF), 1.0, 6.0, ((0, 128),))
    live_panels = plant(jax.random.randint(key_list[1], (NCLUS,), PANELS // 2, PANELS + 1), jax.random.fold_in(key_list[1], 1), PANELS // 2, PANELS).astype(jnp.int32)
    self_blocks = gaussian(key_list[2], (NCLUS, DOF, DOF), DOF ** -0.5, 0.3125, ((0, 128),))
    near_pairs = draw_near_pairs(jax.random.fold_in(key_list[10], 71), 0)
    near_count = draw_near_count(jax.random.fold_in(key_list[10], 71), 0)
    near_blocks = gaussian(key_list[5], (DEVICES * NP_DEV, DOF, DOF), DOF ** -0.5, 0.3125, ((0, 128),))
    far_pairs = draw_far_pairs(jax.random.fold_in(key_list[10], 71), 0)
    far_rank = draw_far_rank(jax.random.fold_in(key_list[10], 71), 0)
    far_left = gaussian(key_list[8], (DEVICES * FP_DEV, DOF, RANK), RANK ** -0.5, 1.0, ((0, 128),))
    far_right = gaussian(key_list[9], (DEVICES * FP_DEV, DOF, RANK), DOF ** -0.5, 0.3125, ((0, 128),))
    return dict(load_vectors=load_vectors, live_panels=live_panels, self_blocks=self_blocks, near_pairs=near_pairs, near_count=near_count, near_blocks=near_blocks, far_pairs=far_pairs, far_rank=far_rank, far_left=far_left, far_right=far_right)


def dof_live(live_panels):
    panel_of = jnp.arange(DOF) % PANELS
    return panel_of[None, :] < live_panels[:, None]


def reference(load_vectors, live_panels, self_blocks, near_pairs, near_count, near_blocks, far_pairs, far_rank, far_left, far_right):
    live_dofs = dof_live(live_panels).astype(jnp.bfloat16)
    masked = load_vectors * live_dofs[:, None, :]
    wide = masked.astype(jnp.float32)
    groups = N_ROW * N_COL
    self_part = jnp.einsum('cld,ced->cle', wide, self_blocks.astype(jnp.float32))

    def one_group(totals, inputs):
        near_ids, near_live, near_mats, far_ids, far_ranks, left_mats, right_mats = inputs
        slot_live = (jnp.arange(NP_DEV) < near_live).astype(jnp.float32)[:, None, None]
        mats = near_mats.astype(jnp.float32)
        rows_in = wide[near_ids[:, 0]]
        cols_in = wide[near_ids[:, 1]]
        to_rows = jnp.einsum('pld,ped->ple', cols_in, mats) * slot_live
        to_cols = jnp.einsum('pld,pde->ple', rows_in, mats) * slot_live
        totals = totals.at[near_ids[:, 0]].add(to_rows)
        totals = totals.at[near_ids[:, 1]].add(to_cols)
        rank_live = (jnp.arange(RANK)[None, :] < far_ranks[:, None]).astype(jnp.float32)[:, None, :]
        left = left_mats.astype(jnp.float32)
        right = right_mats.astype(jnp.float32)
        far_rows_in = wide[far_ids[:, 0]]
        far_cols_in = wide[far_ids[:, 1]]
        proj_cols = (jnp.einsum('pld,pdk->plk', far_cols_in, right) * rank_live).astype(jnp.bfloat16)
        proj_cols = lax.optimization_barrier(proj_cols).astype(jnp.float32)
        proj_rows = (jnp.einsum('pld,pdk->plk', far_rows_in, left) * rank_live).astype(jnp.bfloat16)
        proj_rows = lax.optimization_barrier(proj_rows).astype(jnp.float32)
        far_to_rows = jnp.einsum('plk,pek->ple', proj_cols, left)
        far_to_cols = jnp.einsum('plk,pek->ple', proj_rows, right)
        totals = totals.at[far_ids[:, 0]].add(far_to_rows)
        totals = totals.at[far_ids[:, 1]].add(far_to_cols)
        return totals, None

    inputs = (near_pairs.reshape(groups, NP_DEV, 2), near_count, near_blocks.reshape(groups, NP_DEV, DOF, DOF),
              far_pairs.reshape(groups, FP_DEV, 2), far_rank.reshape(groups, FP_DEV),
              far_left.reshape(groups, FP_DEV, DOF, RANK), far_right.reshape(groups, FP_DEV, DOF, RANK))
    totals, _ = lax.scan(one_group, self_part, inputs)
    return totals * live_dofs.astype(jnp.float32)[:, None, :]
```

```python
import functools

import jax
import jax.numpy as jnp
from jax import lax
from jax.experimental import pallas as pl
from jax.experimental.pallas import tpu as pltpu
from jax.sharding import PartitionSpec as P

NEAR_STEP = 4
FAR_STEP = 8

def pair_kernel(flip, src_of, dst_of, splits, near_pairs, near_count, far_pairs, far_rank, near, proj, back, *refs):
    n_in, n_out = len(splits[0]), len(splits[1])
    sources, outs = refs[:n_in], refs[n_in:n_in + n_out]
    xbuf, nbuf, pbuf, bbuf, acc, obuf, xsem, nsem, psem, bsem, osem = refs[n_in + n_out:]
    near_n, far_n = nbuf.shape[0], far_rank.shape[0]
    spare = acc.shape[0] - 1
    count = near_count[0]
    place = (lax.axis_index("row"), lax.axis_index("col"))
    x_copies, first = [], 0
    for k, size in enumerate(splits[0]):
        x_copies.append(pltpu.make_async_copy(sources[k], xbuf.at[pl.ds(first, size)], xsem.at[k]))
        first += size
    def near_copy(i):
        rows = pl.ds(i * NEAR_STEP, NEAR_STEP)
        return pltpu.make_async_copy(near.at[rows], nbuf.at[rows], nsem.at[i])
    p_copy = pltpu.make_async_copy(proj, pbuf, psem)
    b_copy = pltpu.make_async_copy(back, bbuf, bsem)
    for copy in x_copies:
        copy.start()
    p_copy.start()
    b_copy.start()
    steps = (count + NEAR_STEP - 1) // NEAR_STEP
    @pl.loop(0, acc.shape[0])
    def _(i):
        acc[i] = jnp.zeros(acc.shape[1:], jnp.float32)
    for copy in x_copies:
        copy.wait()
    p_copy.wait()
    b_copy.wait()
    @pl.loop(0, steps)
    def _(i):
        near_copy(i).start()
    rank_n = proj.shape[0] // far_n
    @pl.loop(0, far_n // FAR_STEP)
    def _(i):
        ids = [i * FAR_STEP + u for u in range(FAR_STEP)]
        pairs = [(far_pairs[0, q], far_pairs[1, q], place) for q in ids]
        rows = pl.ds(pl.multiple_of(i * FAR_STEP * rank_n, FAR_STEP * rank_n), FAR_STEP * rank_n)
        x = jnp.concatenate([xbuf[src_of(*pair)] for pair in pairs], axis=0)
        t = lax.dot_general(x, pbuf[rows], (((1,), (1,)), ((), ())), preferred_element_type=jnp.float32)
        lane = lax.broadcasted_iota(jnp.int32, (xbuf.shape[1], FAR_STEP * rank_n), 1)
        parts = []
        for u, q in enumerate(ids):
            keep = (lane >= u * rank_n) & (lane < u * rank_n + far_rank[q])
            parts.append(jnp.where(keep, t[u * xbuf.shape[1]:(u + 1) * xbuf.shape[1]], 0.0).astype(jnp.bfloat16))
        y = jnp.dot(jnp.concatenate(parts, axis=0), bbuf[rows], preferred_element_type=jnp.float32)
        for u, pair in enumerate(pairs):
            acc[dst_of(*pair)] += y[u * xbuf.shape[1]:(u + 1) * xbuf.shape[1]]
    @pl.loop(0, steps)
    def _(i):
        near_copy(i).wait()
        for u in range(NEAR_STEP):
            p = i * NEAR_STEP + u
            src = src_of(near_pairs[0, p], near_pairs[1, p], place)
            dst = dst_of(near_pairs[0, p], near_pairs[1, p], place)
            dst = jnp.where(p < count, dst, spare)
            dims = (((1,), (1,)), ((), ())) if flip else (((1,), (0,)), ((), ()))
            acc[dst] += lax.dot_general(xbuf[src], nbuf[p], dims, preferred_element_type=jnp.float32)
    o_copies, first = [], 0
    for k, size in enumerate(splits[1]):
        @pl.loop(first, first + size)
        def _(i):
            obuf[i] = acc[i].astype(jnp.bfloat16)
        copy = pltpu.make_async_copy(obuf.at[pl.ds(first, size)], outs[k], osem.at[k])
        copy.start()
        o_copies.append(copy)
        first += size
    for copy in o_copies:
        copy.wait()

def pair_product(flip, src_of, dst_of, in_sizes, out_sizes, near_pairs, near_count, far_pairs, far_rank, near, proj, back, sources):
    loads, dof = sources[0].shape[1:]
    smem = pl.BlockSpec(memory_space=pltpu.SMEM)
    hbm = pl.BlockSpec(memory_space=pl.ANY)
    n_dst = sum(out_sizes)
    near_n = near.shape[0]
    return pl.pallas_call(
        functools.partial(pair_kernel, flip, src_of, dst_of, (in_sizes, out_sizes)),
        out_shape=[jax.ShapeDtypeStruct((n, loads, dof), jnp.bfloat16) for n in out_sizes],
        in_specs=[smem] * 4 + [hbm] * (3 + len(sources)),
        out_specs=[hbm] * len(out_sizes),
        scratch_shapes=[
            pltpu.VMEM((sum(in_sizes), loads, dof), jnp.bfloat16),
            pltpu.VMEM(near.shape, jnp.bfloat16),
            pltpu.VMEM(proj.shape, jnp.bfloat16),
            pltpu.VMEM(back.shape, jnp.bfloat16),
            pltpu.VMEM((n_dst + 1, loads, dof), jnp.float32),
            pltpu.VMEM((n_dst, loads, dof), jnp.bfloat16),
            pltpu.SemaphoreType.DMA((len(sources),)),
            pltpu.SemaphoreType.DMA((near_n // NEAR_STEP,)),
            pltpu.SemaphoreType.DMA,
            pltpu.SemaphoreType.DMA,
            pltpu.SemaphoreType.DMA((len(out_sizes),)),
        ],
        compiler_params=pltpu.CompilerParams(vmem_limit_bytes=58 * 2**20),
        cost_estimate=pl.CostEstimate(flops=2 * near_n * loads * dof * dof, bytes_accessed=2 * near.size + 4 * proj.size, transcendentals=0),
    )(near_pairs, near_count, far_pairs, far_rank, near, proj, back, *sources)


SIDE = 4
PER = 8


def row_shift(axis, step):
    pairs = []
    for y in range(SIDE):
        for z in range(SIDE):
            far = ((y + step) % SIDE, z) if axis == 0 else (y, (z + step) % SIDE)
            pairs.append((far[0] * SIDE + far[1], y * SIDE + z))
    return pairs


def col_shift(step, other):
    return [((x + step) % SIDE * 2 + (core ^ other), x * 2 + core) for x in range(SIDE) for core in range(2)]


def row_slot(r, place):
    piece = (r // PER) % (2 * SIDE)
    step = (piece // 2 - place[1] // 2 + SIDE) % SIDE
    return step, (piece % 2) ^ (place[1] % 2), r % PER


def src_rows(r, c, place):
    step, other, j = row_slot(r, place)
    return (step * 2 + other) * PER + j


def dst_rows(r, c, place):
    step, other, j = row_slot(r, place)
    return ((1 - other) * SIDE + step) * PER + j


def src_cols(r, c, place):
    return c // (2 * SIDE * PER) * PER + c % PER


HALF_AT = sum(at << (4 * i) for i, at in enumerate((6, 7, 4, 1, 0, 2, 3, 5)))
RING_OUT = (16, 16, 8, 8, 16)


def dst_cols(r, c, place):
    piece = c // (2 * SIDE * PER)
    dy = (piece // SIDE - place[0] // SIDE + SIDE) % SIDE
    dz = (piece % SIDE - place[0] % SIDE + SIDE) % SIDE
    j = c % PER
    late, half, low = j // 4, (j // 2) % 2, j % 2
    first = jnp.where(late == 0, dz, dy)
    second = jnp.where(late == 0, dy, dz)
    at = lax.shift_right_logical(jnp.int32(HALF_AT - (1 << 32) if HALF_AT >= 1 << 31 else HALF_AT), (first * 2 + half) * 4) & 15
    return late * 64 + at * 8 + second * 2 + low


def wide(v):
    return v.astype(jnp.float32)


def narrow(v):
    return v.astype(jnp.bfloat16)


def ring_sum(parts, axis):
    forth, back, forth_own, back_own, own = parts
    go = lambda v, ax, step: lax.ppermute(v, "row", row_shift(ax, step))
    from_low = go(forth, axis, -1)
    from_high = go(back, axis, 1)
    low_two = go(narrow(wide(forth_own) + wide(from_low[:8])), axis, -1)
    high_two = go(narrow(wide(back_own) + wide(from_high[:8])), axis, 1)
    one = wide(own[:8]) + wide(low_two) + wide(from_high[8:])
    two = wide(own[8:]) + wide(from_low[8:]) + wide(high_two)
    block = lambda d: jnp.concatenate([one[2 * d:2 * d + 2], two[2 * d:2 * d + 2]])
    ax = 1 - axis
    return (
        block(0)
        + wide(go(narrow(block(1)), ax, -1))
        + wide(go(narrow(block(2)), ax, 2))
        + wide(go(narrow(block(3)), ax, 1))
    )


def local(
    load_vectors,
    live_panels,
    self_blocks,
    near_pairs,
    near_count,
    near_blocks,
    far_pairs,
    far_rank,
    far_left,
    far_right,
):
    dof = load_vectors.shape[2]
    panel_of = jnp.arange(dof) % (dof // 3)
    live_dofs = (panel_of[None, :] < live_panels[:, None]).astype(jnp.bfloat16)
    masked = load_vectors * live_dofs[:, None, :]
    col_block = lax.all_gather(masked, "row", axis=0, tiled=True)
    swap = lambda v: lax.ppermute(v, "col", col_shift(0, 1))
    rows = []
    for step in range(SIDE):
        there = masked if step == 0 else lax.ppermute(masked, "col", col_shift(step, 0))
        rows += [there, swap(there)]
    left = jnp.swapaxes(far_left, 1, 2).reshape(-1, dof)
    right = jnp.swapaxes(far_right, 1, 2).reshape(-1, dof)
    lists = (near_pairs.T, near_count, far_pairs.T, far_rank, near_blocks)
    to_cols = pair_product(False, src_rows, dst_cols, [PER] * 8, RING_OUT * 2, *lists, left, right, rows)
    to_rows = pair_product(
        True, src_cols, dst_rows, [PER * SIDE * SIDE], (PER * SIDE, PER * SIDE), *lists, right, left, [col_block]
    )
    early = ring_sum(to_cols[:5], 1)
    late = ring_sum(to_cols[5:], 0)
    col_part = jnp.concatenate([early, late])
    row_sum = (wide(to_rows[1]) + wide(swap(to_rows[0]))).reshape((SIDE, PER) + masked.shape[1:])
    row_part = row_sum[0]
    for step in range(1, SIDE):
        row_part = row_part + wide(lax.ppermute(narrow(row_sum[step]), "col", col_shift(-step, 0)))
    own_part = jnp.einsum("cld,ced->cle", masked, self_blocks, preferred_element_type=jnp.float32)
    return (own_part + row_part + col_part) * live_dofs.astype(jnp.float32)[:, None, :]


def solution(mesh):
    spec = P(("row", "col"))
    return jax.shard_map(local, mesh=mesh, in_specs=(spec,) * 10, out_specs=spec, check_vma=False)
```

```python
import functools

import jax
import jax.numpy as jnp
from jax import lax
from jax.experimental import pallas as pl
from jax.experimental.pallas import tpu as pltpu
from jax.sharding import PartitionSpec as P

NEAR_STEP = 4
FAR_STEP = 8

def pair_kernel(flip, src_of, dst_of, splits, near_pairs, near_count, far_pairs, far_rank, near, proj, back, *refs):
    n_in, n_out = len(refs) - 11 - len(splits[1]), len(splits[1])
    sources, outs = refs[:n_in], refs[n_in:n_in + n_out]
    xbuf, nbuf, pbuf, bbuf, acc, obuf, xsem, nsem, psem, bsem, osem = refs[n_in + n_out:]
    near_n, far_n = nbuf.shape[0], far_rank.shape[0]
    spare = acc.shape[0] - 1
    count = near_count[0]
    place = (lax.axis_index("row"), lax.axis_index("col"))
    x_copies, first = [], 0
    for n, (k, where, size) in enumerate(splits[0]):
        source = sources[k] if where is None else sources[k].at[where]
        x_copies.append(pltpu.make_async_copy(source, xbuf.at[pl.ds(first, size)], xsem.at[n]))
        first += size
    def near_copy(i):
        rows = pl.ds(i * NEAR_STEP, NEAR_STEP)
        return pltpu.make_async_copy(near.at[rows], nbuf.at[rows], nsem.at[i])
    p_copy = pltpu.make_async_copy(proj, pbuf, psem)
    b_copy = pltpu.make_async_copy(back, bbuf, bsem)
    for copy in x_copies:
        copy.start()
    p_copy.start()
    b_copy.start()
    steps = (count + NEAR_STEP - 1) // NEAR_STEP
    @pl.loop(0, acc.shape[0])
    def _(i):
        acc[i] = jnp.zeros(acc.shape[1:], jnp.float32)
    for copy in x_copies:
        copy.wait()
    p_copy.wait()
    b_copy.wait()
    @pl.loop(0, steps)
    def _(i):
        near_copy(i).start()
    rank_n = proj.shape[0] // far_n
    @pl.loop(0, far_n // FAR_STEP)
    def _(i):
        ids = [i * FAR_STEP + u for u in range(FAR_STEP)]
        pairs = [(far_pairs[0, q], far_pairs[1, q], place) for q in ids]
        rows = pl.ds(pl.multiple_of(i * FAR_STEP * rank_n, FAR_STEP * rank_n), FAR_STEP * rank_n)
        x = jnp.concatenate([xbuf[src_of(*pair)] for pair in pairs], axis=0)
        t = lax.dot_general(x, pbuf[rows], (((1,), (1,)), ((), ())), preferred_element_type=jnp.float32)
        lane = lax.broadcasted_iota(jnp.int32, (xbuf.shape[1], FAR_STEP * rank_n), 1)
        parts = []
        for u, q in enumerate(ids):
            keep = (lane >= u * rank_n) & (lane < u * rank_n + far_rank[q])
            parts.append(jnp.where(keep, t[u * xbuf.shape[1]:(u + 1) * xbuf.shape[1]], 0.0).astype(jnp.bfloat16))
        y = jnp.dot(jnp.concatenate(parts, axis=0), bbuf[rows], preferred_element_type=jnp.float32)
        for u, pair in enumerate(pairs):
            acc[dst_of(*pair)] += y[u * xbuf.shape[1]:(u + 1) * xbuf.shape[1]]
    @pl.loop(0, steps)
    def _(i):
        near_copy(i).wait()
        for u in range(NEAR_STEP):
            p = i * NEAR_STEP + u
            src = src_of(near_pairs[0, p], near_pairs[1, p], place)
            dst = dst_of(near_pairs[0, p], near_pairs[1, p], place)
            dst = jnp.where(p < count, dst, spare)
            dims = (((1,), (1,)), ((), ())) if flip else (((1,), (0,)), ((), ()))
            acc[dst] += lax.dot_general(xbuf[src], nbuf[p], dims, preferred_element_type=jnp.float32)
    o_copies, first = [], 0
    for k, size in enumerate(splits[1]):
        @pl.loop(first, first + size)
        def _(i):
            obuf[i] = acc[i].astype(jnp.bfloat16)
        copy = pltpu.make_async_copy(obuf.at[pl.ds(first, size)], outs[k], osem.at[k])
        copy.start()
        o_copies.append(copy)
        first += size
    for copy in o_copies:
        copy.wait()

def pair_product(flip, vmem_mib, src_of, dst_of, in_sizes, out_sizes, near_pairs, near_count, far_pairs, far_rank, near, proj, back, sources):
    loads, dof = sources[0].shape[-2:]
    smem = pl.BlockSpec(memory_space=pltpu.SMEM)
    hbm = pl.BlockSpec(memory_space=pl.ANY)
    n_dst = sum(out_sizes)
    near_n = near.shape[0]
    return pl.pallas_call(
        functools.partial(pair_kernel, flip, src_of, dst_of, (in_sizes, out_sizes)),
        out_shape=[jax.ShapeDtypeStruct((n, loads, dof), jnp.bfloat16) for n in out_sizes],
        in_specs=[smem] * 4 + [hbm] * (3 + len(sources)),
        out_specs=[hbm] * len(out_sizes),
        scratch_shapes=[
            pltpu.VMEM((sum(size for _, _, size in in_sizes), loads, dof), jnp.bfloat16),
            pltpu.VMEM(near.shape, jnp.bfloat16),
            pltpu.VMEM(proj.shape, jnp.bfloat16),
            pltpu.VMEM(back.shape, jnp.bfloat16),
            pltpu.VMEM((n_dst + 1, loads, dof), jnp.float32),
            pltpu.VMEM((n_dst, loads, dof), jnp.bfloat16),
            pltpu.SemaphoreType.DMA((len(in_sizes),)),
            pltpu.SemaphoreType.DMA((near_n // NEAR_STEP,)),
            pltpu.SemaphoreType.DMA,
            pltpu.SemaphoreType.DMA,
            pltpu.SemaphoreType.DMA((len(out_sizes),)),
        ],
        compiler_params=pltpu.CompilerParams(vmem_limit_bytes=vmem_mib * 2**20),
        cost_estimate=pl.CostEstimate(flops=2 * near_n * loads * dof * dof, bytes_accessed=2 * near.size + 4 * proj.size, transcendentals=0),
    )(near_pairs, near_count, far_pairs, far_rank, near, proj, back, *sources)


SIDE = 4
PER = 8


def col_shift(step, other):
    return [((x + step) % SIDE * 2 + (core ^ other), x * 2 + core) for x in range(SIDE) for core in range(2)]


def plane_shift(first, step):
    pairs = []
    for y in range(SIDE):
        for z in range(SIDE):
            for col in range(2 * SIDE):
                along_y = (col % 2 == 0) == (first == 1)
                far = ((y + step) % SIDE, z) if along_y else (y, (z + step) % SIDE)
                pairs.append(((far[0] * SIDE + far[1]) * 2 * SIDE + col, (y * SIDE + z) * 2 * SIDE + col))
    return pairs


def row_place(r, place):
    piece = (r // PER) % (2 * SIDE)
    return (piece // 2 - place[1] // 2 + SIDE) % SIDE, (piece % 2) ^ (place[1] % 2), r % PER


def src_rows(r, c, place):
    step, other, j = row_place(r, place)
    near_step = jnp.where(place[1] % 2 == 0, SIDE - 1, 1)
    at = jnp.where(step == 0, other, jnp.where(step == 2, 6 + other, jnp.where(step == near_step, 2 + other, 5 - other)))
    return at * PER + j


def dst_rows(r, c, place):
    step, other, j = row_place(r, place)
    mine = (step == jnp.where(place[1] % 2 == 0, 1, SIDE - 1)) | ((step % 2 == 0) & (other == 0))
    at = jnp.where(step == 0, 3, jnp.where(step == 2, 2, jnp.where(mine, other, 1 - other)))
    return (jnp.where(mine, SIDE, 0) + at) * PER + j


def col_place(c, place):
    piece = c // (2 * SIDE * PER)
    dy = (piece // SIDE - place[0] // SIDE + SIDE) % SIDE
    dz = (piece % SIDE - place[0] % SIDE + SIDE) % SIDE
    j = c % PER
    late = j // 4
    return jnp.where(late == 0, dz, dy), jnp.where(late == 0, dy, dz), late, j % 4


def src_cols(r, c, place):
    first, second, late, j = col_place(c, place)
    return (late ^ (place[1] % 2)) * 64 + first * 16 + second * 4 + j


def dst_cols(r, c, place):
    first, second, late, j = col_place(c, place)
    return (late ^ (place[1] % 2)) * 64 + (first + SIDE - 1) % SIDE * 16 + second * 4 + j


def wide(v):
    return v.astype(jnp.float32)


def narrow(v):
    return v.astype(jnp.bfloat16)


def swap(v):
    return lax.ppermute(v, "col", col_shift(0, 1))


def local(
    load_vectors,
    live_panels,
    self_blocks,
    near_pairs,
    near_count,
    near_blocks,
    far_pairs,
    far_rank,
    far_left,
    far_right,
):
    dof = load_vectors.shape[2]
    panel_of = jnp.arange(dof) % (dof // 3)
    live_dofs = (panel_of[None, :] < live_panels[:, None]).astype(jnp.bfloat16)
    masked = load_vectors * live_dofs[:, None, :]
    core = lax.axis_index("col") % 2
    twin = swap(masked)
    part = lambda v: lax.dynamic_slice_in_dim(v, core * (PER // 2), PER // 2)
    own = jnp.stack([part(masked), part(twin)])
    plane = lambda v, first, step: lax.ppermute(v, ("row", "col"), plane_shift(first, step))
    chip = [((x - 1 + 2 * core) % SIDE * 2 + core, x * 2 + core) for x in range(SIDE) for core in range(2)]
    x_near = lax.ppermute(masked, "col", chip)
    x_cross = lax.ppermute(twin, "col", chip)
    line = [plane(own, 1, step) for step in (1, 3, 2)]
    x_two = lax.ppermute(x_near, "col", chip)
    x_near, x_cross, x_two, line = lax.optimization_barrier((x_near, x_cross, x_two, line))
    line = jnp.stack([own, line[0], line[2], line[1]])
    cols = [line] + [plane(line, 0, step) for step in (1, 2, 3)]
    rows = [masked, twin, x_near, x_cross, swap(x_near), swap(x_cross), x_two, swap(x_two)]
    left = jnp.swapaxes(far_left, 1, 2).reshape(-1, dof)
    right = jnp.swapaxes(far_right, 1, 2).reshape(-1, dof)
    lists = (near_pairs.T, near_count, far_pairs.T, far_rank, near_blocks)
    to_cols = pair_product(False, 44, src_rows, dst_cols, [(k, None, n) for k, n in enumerate((8,) * 8)], (16, 16, 16, 16, 24, 24, 16), *lists, left, right, rows)
    theirs = [swap(to_cols[4]), swap(to_cols[5])]
    cols[1:], theirs = lax.optimization_barrier((cols[1:], theirs))
    theirs = [theirs[0][:16], jnp.concatenate([theirs[0][16:], theirs[1][:8]]), theirs[1][8:], swap(to_cols[6])]
    sums = [jnp.stack([to_cols[k], theirs[k]]) for k in range(SIDE)]
    cols += [swap(v[:, 1]) for v in cols]
    sums_in = [plane(sums[step - 1], 0, -step) for step in (1, 2, 3)]
    pieces = [(k, (at, 0) if k < 4 else at, 4) for k in range(8) for at in range(SIDE)]
    to_rows = pair_product(True, 38, src_cols, dst_rows, pieces, (16,) * 4, *lists, right, left, cols)
    row_near = wide(to_rows[2]) + wide(swap(to_rows[0]))
    row_far = wide(to_rows[3]) + wide(swap(to_rows[1]))
    row_near, row_far, sums_in = lax.optimization_barrier((row_near, row_far, sums_in))
    forth = lax.ppermute(narrow(jnp.concatenate([row_far[:PER], row_near[PER:]])), "col", chip)
    line_sum = (wide(sums[3]) + sum(wide(v) for v in sums_in)).reshape((2, SIDE, PER // 2) + masked.shape[1:])
    ends = [plane(narrow(line_sum[:, step]), 1, -step) for step in (1, 2, 3)]
    forth, ends = lax.optimization_barrier((forth, ends))
    forth_two = lax.ppermute(narrow(row_near[:PER] + wide(forth[:PER])), "col", chip)
    row_part = [row_far[PER:], swap(forth[PER:]), forth_two]
    end = line_sum[:, 0] + sum(wide(v) for v in ends)
    end_in = swap(end[1])
    col_part = jnp.where(core == 0, jnp.concatenate([end[0], end_in]), jnp.concatenate([end_in, end[0]]))
    own_part = jnp.einsum("cld,ced->cle", masked, self_blocks, preferred_element_type=jnp.float32)
    total = own_part + sum(wide(v) for v in row_part) + col_part
    return total * live_dofs.astype(jnp.float32)[:, None, :]


def solution(mesh):
    spec = P(("row", "col"))
    return jax.shard_map(local, mesh=mesh, in_specs=(spec,) * 10, out_specs=spec, check_vma=False)
```

```python
import functools

import jax
import jax.numpy as jnp
from jax import lax
from jax.experimental import pallas as pl
from jax.experimental.pallas import tpu as pltpu
from jax.sharding import PartitionSpec as P

NEAR_STEP = 4
FAR_STEP = 8

def pair_kernel(flip, src_of, dst_of, splits, near_pairs, near_count, far_pairs, far_rank, near, proj, back, *refs):
    n_in, n_out = len(refs) - 11 - len(splits[1]), len(splits[1])
    sources, outs = refs[:n_in], refs[n_in:n_in + n_out]
    xbuf, nbuf, pbuf, bbuf, acc, obuf, xsem, nsem, psem, bsem, osem = refs[n_in + n_out:]
    near_n, far_n = nbuf.shape[0], far_rank.shape[0]
    spare = acc.shape[0] - 1
    count = near_count[0]
    place = (lax.axis_index("row"), lax.axis_index("col"))
    x_copies, first = [], 0
    for n, (k, where, size) in enumerate(splits[0]):
        source = sources[k] if where is None else sources[k].at[where]
        x_copies.append(pltpu.make_async_copy(source, xbuf.at[pl.ds(first, size)], xsem.at[n]))
        first += size
    def near_copy(i):
        rows = pl.ds(i * NEAR_STEP, NEAR_STEP)
        return pltpu.make_async_copy(near.at[rows], nbuf.at[rows], nsem.at[i])
    p_copy = pltpu.make_async_copy(proj, pbuf, psem)
    b_copy = pltpu.make_async_copy(back, bbuf, bsem)
    for copy in x_copies:
        copy.start()
    p_copy.start()
    b_copy.start()
    steps = (count + NEAR_STEP - 1) // NEAR_STEP
    @pl.loop(0, acc.shape[0])
    def _(i):
        acc[i] = jnp.zeros(acc.shape[1:], jnp.float32)
    for copy in x_copies:
        copy.wait()
    p_copy.wait()
    b_copy.wait()
    @pl.loop(0, steps)
    def _(i):
        near_copy(i).start()
    rank_n = proj.shape[0] // far_n
    @pl.loop(0, far_n // FAR_STEP)
    def _(i):
        ids = [i * FAR_STEP + u for u in range(FAR_STEP)]
        pairs = [(far_pairs[0, q], far_pairs[1, q], place) for q in ids]
        rows = pl.ds(pl.multiple_of(i * FAR_STEP * rank_n, FAR_STEP * rank_n), FAR_STEP * rank_n)
        x = jnp.concatenate([xbuf[src_of(*pair)] for pair in pairs], axis=0)
        t = lax.dot_general(x, pbuf[rows], (((1,), (1,)), ((), ())), preferred_element_type=jnp.float32)
        lane = lax.broadcasted_iota(jnp.int32, (xbuf.shape[1], FAR_STEP * rank_n), 1)
        parts = []
        for u, q in enumerate(ids):
            keep = (lane >= u * rank_n) & (lane < u * rank_n + far_rank[q])
            parts.append(jnp.where(keep, t[u * xbuf.shape[1]:(u + 1) * xbuf.shape[1]], 0.0).astype(jnp.bfloat16))
        y = jnp.dot(jnp.concatenate(parts, axis=0), bbuf[rows], preferred_element_type=jnp.float32)
        for u, pair in enumerate(pairs):
            acc[dst_of(*pair)] += y[u * xbuf.shape[1]:(u + 1) * xbuf.shape[1]]
    @pl.loop(0, steps)
    def _(i):
        near_copy(i).wait()
        for u in range(NEAR_STEP):
            p = i * NEAR_STEP + u
            src = src_of(near_pairs[0, p], near_pairs[1, p], place)
            dst = dst_of(near_pairs[0, p], near_pairs[1, p], place)
            dst = jnp.where(p < count, dst, spare)
            dims = (((1,), (1,)), ((), ())) if flip else (((1,), (0,)), ((), ()))
            acc[dst] += lax.dot_general(xbuf[src], nbuf[p], dims, preferred_element_type=jnp.float32)
    o_copies, first = [], 0
    for k, size in enumerate(splits[1]):
        @pl.loop(first, first + size)
        def _(i):
            obuf[i] = acc[i].astype(jnp.bfloat16)
        copy = pltpu.make_async_copy(obuf.at[pl.ds(first, size)], outs[k], osem.at[k])
        copy.start()
        o_copies.append(copy)
        first += size
    for copy in o_copies:
        copy.wait()

def pair_product(flip, vmem_mib, src_of, dst_of, in_sizes, out_sizes, near_pairs, near_count, far_pairs, far_rank, near, proj, back, sources):
    loads, dof = sources[0].shape[-2:]
    smem = pl.BlockSpec(memory_space=pltpu.SMEM)
    hbm = pl.BlockSpec(memory_space=pl.ANY)
    n_dst = sum(out_sizes)
    near_n = near.shape[0]
    return pl.pallas_call(
        functools.partial(pair_kernel, flip, src_of, dst_of, (in_sizes, out_sizes)),
        out_shape=[jax.ShapeDtypeStruct((n, loads, dof), jnp.bfloat16) for n in out_sizes],
        in_specs=[smem] * 4 + [hbm] * (3 + len(sources)),
        out_specs=[hbm] * len(out_sizes),
        scratch_shapes=[
            pltpu.VMEM((sum(size for _, _, size in in_sizes), loads, dof), jnp.bfloat16),
            pltpu.VMEM(near.shape, jnp.bfloat16),
            pltpu.VMEM(proj.shape, jnp.bfloat16),
            pltpu.VMEM(back.shape, jnp.bfloat16),
            pltpu.VMEM((n_dst + 1, loads, dof), jnp.float32),
            pltpu.VMEM((n_dst, loads, dof), jnp.bfloat16),
            pltpu.SemaphoreType.DMA((len(in_sizes),)),
            pltpu.SemaphoreType.DMA((near_n // NEAR_STEP,)),
            pltpu.SemaphoreType.DMA,
            pltpu.SemaphoreType.DMA,
            pltpu.SemaphoreType.DMA((len(out_sizes),)),
        ],
        compiler_params=pltpu.CompilerParams(vmem_limit_bytes=vmem_mib * 2**20),
        cost_estimate=pl.CostEstimate(flops=2 * near_n * loads * dof * dof, bytes_accessed=2 * near.size + 4 * proj.size, transcendentals=0),
    )(near_pairs, near_count, far_pairs, far_rank, near, proj, back, *sources)


SIDE = 4
PER = 8


def col_shift(step, other):
    return [((x + step) % SIDE * 2 + (core ^ other), x * 2 + core) for x in range(SIDE) for core in range(2)]


def plane_shift(first, step):
    pairs = []
    for y in range(SIDE):
        for z in range(SIDE):
            for col in range(2 * SIDE):
                along_y = (col % 2 == 0) == (first == 1)
                far = ((y + step) % SIDE, z) if along_y else (y, (z + step) % SIDE)
                pairs.append(((far[0] * SIDE + far[1]) * 2 * SIDE + col, (y * SIDE + z) * 2 * SIDE + col))
    return pairs


def row_place(r, place):
    piece = (r // PER) % (2 * SIDE)
    return (piece // 2 - place[1] // 2 + SIDE) % SIDE, (piece % 2) ^ (place[1] % 2), r % PER


def src_rows(r, c, place):
    step, other, j = row_place(r, place)
    near_step = jnp.where(place[1] % 2 == 0, SIDE - 1, 1)
    at = jnp.where(step == 0, other, jnp.where(step == 2, 6 + other, jnp.where(step == near_step, 2 + other, 5 - other)))
    return at * PER + j


def dst_rows(r, c, place):
    step, other, j = row_place(r, place)
    mine = (step == jnp.where(place[1] % 2 == 0, 1, SIDE - 1)) | ((step % 2 == 0) & (other == 0))
    at = jnp.where(step == 0, 3, jnp.where(step == 2, 2, jnp.where(mine, other, 1 - other)))
    return (jnp.where(mine, SIDE, 0) + at) * PER + j


def col_place(c, place):
    piece = c // (2 * SIDE * PER)
    dy = (piece // SIDE - place[0] // SIDE + SIDE) % SIDE
    dz = (piece % SIDE - place[0] % SIDE + SIDE) % SIDE
    j = c % PER
    late = j // 4
    return jnp.where(late == 0, dz, dy), jnp.where(late == 0, dy, dz), late, j % 4


def src_cols(r, c, place):
    first, second, late, j = col_place(c, place)
    return (late ^ (place[1] % 2)) * 64 + first * 16 + second * 4 + j


def dst_cols(r, c, place):
    first, second, late, j = col_place(c, place)
    return (late ^ (place[1] % 2)) * 64 + (first + SIDE - 1) % SIDE * 16 + second * 4 + j


def wide(v):
    return v.astype(jnp.float32)


def narrow(v):
    return v.astype(jnp.bfloat16)


def swap(v):
    return lax.ppermute(v, "col", col_shift(0, 1))


def local(
    load_vectors,
    live_panels,
    self_blocks,
    near_pairs,
    near_count,
    near_blocks,
    far_pairs,
    far_rank,
    far_left,
    far_right,
):
    dof = load_vectors.shape[2]
    panel_of = jnp.arange(dof) % (dof // 3)
    masked = load_vectors * (panel_of[None, :] < live_panels[:, None]).astype(jnp.bfloat16)[:, None, :]
    core = lax.axis_index("col") % 2
    twin = swap(masked)
    part = lambda v: lax.dynamic_slice_in_dim(v, core * (PER // 2), PER // 2)
    own = jnp.stack([part(masked), part(twin)])
    plane = lambda v, first, step: lax.ppermute(v, ("row", "col"), plane_shift(first, step))
    chip = [((x - 1 + 2 * core) % SIDE * 2 + core, x * 2 + core) for x in range(SIDE) for core in range(2)]
    x_near = lax.ppermute(masked, "col", chip)
    x_cross = lax.ppermute(twin, "col", chip)
    line = [plane(own, 1, step) for step in (1, 3, 2)]
    x_two = lax.ppermute(x_near, "col", chip)
    x_near, x_cross, line = lax.optimization_barrier((x_near, x_cross, line))
    line = jnp.stack([own, line[0], line[2], line[1]])
    cols = [line] + [plane(line, 0, step) for step in (1, 2, 3)]
    rows = [masked, twin, x_near, x_cross, swap(x_near), swap(x_cross), x_two, swap(x_two)]
    left = jnp.swapaxes(far_left, 1, 2).reshape(-1, dof)
    right = jnp.swapaxes(far_right, 1, 2).reshape(-1, dof)
    lists = (near_pairs.T, near_count, far_pairs.T, far_rank, near_blocks)
    to_cols = pair_product(False, 44, src_rows, dst_cols, [(k, None, n) for k, n in enumerate((8,) * 8)], (16, 16, 16, 16, 24, 24, 16), *lists, left, right, rows)
    theirs = [swap(to_cols[4]), swap(to_cols[5])]
    cols[1:], theirs = lax.optimization_barrier((cols[1:], theirs))
    theirs = [theirs[0][:16], jnp.concatenate([theirs[0][16:], theirs[1][:8]]), theirs[1][8:], swap(to_cols[6])]
    sums = [jnp.stack([to_cols[k], theirs[k]]) for k in range(SIDE)]
    cols += [swap(v[:, 1]) for v in cols]
    sums_in = [plane(sums[step - 1], 0, -step) for step in (1, 2, 3)]
    pieces = [(k, (at, 0) if k < 4 else at, 4) for k in range(8) for at in range(SIDE)]
    to_rows = pair_product(True, 38, src_cols, dst_rows, pieces, (16,) * 4, *lists, right, left, cols)
    row_near = wide(to_rows[2]) + wide(swap(to_rows[0]))
    row_far = wide(to_rows[3]) + wide(swap(to_rows[1]))
    row_near, row_far, sums_in = lax.optimization_barrier((row_near, row_far, sums_in))
    forth = lax.ppermute(narrow(row_far[:PER]), "col", chip)
    cross = lax.ppermute(narrow(row_near[PER:]), "col", chip)
    split = lambda v: v.reshape((2, SIDE, PER // 2) + masked.shape[1:])
    line_in = [split(v) for v in [sums[3], *sums_in]]
    block = lambda step: sum(wide(v[:, step]) for v in line_in)
    ends = [plane(narrow(block(step)), 1, -step) for step in (1, 2, 3)]
    forth_two = lax.ppermute(narrow(row_near[:PER] + wide(forth)), "col", chip)
    forth_two, ends = lax.optimization_barrier((forth_two, ends))
    end = block(0)
    end_in = wide(swap(narrow(end[1] + sum(wide(v[1]) for v in ends))))
    end_own = end[0] + sum(wide(v[0]) for v in ends)
    own_part = jnp.einsum("cld,ced->cle", masked, self_blocks, preferred_element_type=jnp.float32)
    base = own_part + row_far[PER:] + wide(swap(cross)) + wide(forth_two)
    base, end_in = lax.optimization_barrier((base, end_in))
    total = base + jnp.where(core == 0, jnp.concatenate([end_own, end_in]), jnp.concatenate([end_in, end_own]))
    live_out = (panel_of[None, :] < lax.optimization_barrier(live_panels)[:, None]).astype(jnp.float32)
    return total * live_out[:, None, :]


def solution(mesh):
    spec = P(("row", "col"))
    return jax.shard_map(local, mesh=mesh, in_specs=(spec,) * 10, out_specs=spec, check_vma=False)
```

```python
import functools

import jax
import jax.numpy as jnp
from jax import lax
from jax.experimental import pallas as pl
from jax.experimental.pallas import tpu as pltpu
from jax.sharding import PartitionSpec as P

NEAR_STEP = 4
FAR_STEP = 8

def pair_kernel(flip, src_of, dst_of, splits, near_pairs, near_count, far_pairs, far_rank, near, proj, back, *refs):
    n_in, n_out = len(refs) - 11 - len(splits[1]), len(splits[1])
    sources, outs = refs[:n_in], refs[n_in:n_in + n_out]
    xbuf, nbuf, pbuf, bbuf, acc, obuf, xsem, nsem, psem, bsem, osem = refs[n_in + n_out:]
    near_n, far_n = nbuf.shape[0], far_rank.shape[0]
    spare = acc.shape[0] - 1
    count = near_count[0]
    place = (lax.axis_index("row"), lax.axis_index("col"))
    x_copies, first = [], 0
    for n, (k, where, size) in enumerate(splits[0]):
        source = sources[k] if where is None else sources[k].at[where]
        x_copies.append(pltpu.make_async_copy(source, xbuf.at[pl.ds(first, size)], xsem.at[n]))
        first += size
    def near_copy(i):
        rows = pl.ds(i * NEAR_STEP, NEAR_STEP)
        return pltpu.make_async_copy(near.at[rows], nbuf.at[rows], nsem.at[i])
    p_copy = pltpu.make_async_copy(proj, pbuf, psem)
    b_copy = pltpu.make_async_copy(back, bbuf, bsem)
    for copy in x_copies:
        copy.start()
    p_copy.start()
    b_copy.start()
    steps = (count + NEAR_STEP - 1) // NEAR_STEP
    @pl.loop(0, acc.shape[0])
    def _(i):
        acc[i] = jnp.zeros(acc.shape[1:], jnp.float32)
    for copy in x_copies:
        copy.wait()
    p_copy.wait()
    b_copy.wait()
    @pl.loop(0, steps)
    def _(i):
        near_copy(i).start()
    rank_n = proj.shape[0] // far_n
    @pl.loop(0, far_n // FAR_STEP)
    def _(i):
        ids = [i * FAR_STEP + u for u in range(FAR_STEP)]
        pairs = [(far_pairs[0, q], far_pairs[1, q], place) for q in ids]
        rows = pl.ds(pl.multiple_of(i * FAR_STEP * rank_n, FAR_STEP * rank_n), FAR_STEP * rank_n)
        x = jnp.concatenate([xbuf[src_of(*pair)] for pair in pairs], axis=0)
        t = lax.dot_general(x, pbuf[rows], (((1,), (1,)), ((), ())), preferred_element_type=jnp.float32)
        lane = lax.broadcasted_iota(jnp.int32, (xbuf.shape[1], FAR_STEP * rank_n), 1)
        parts = []
        for u, q in enumerate(ids):
            keep = (lane >= u * rank_n) & (lane < u * rank_n + far_rank[q])
            parts.append(jnp.where(keep, t[u * xbuf.shape[1]:(u + 1) * xbuf.shape[1]], 0.0).astype(jnp.bfloat16))
        y = jnp.dot(jnp.concatenate(parts, axis=0), bbuf[rows], preferred_element_type=jnp.float32)
        for u, pair in enumerate(pairs):
            acc[dst_of(*pair)] += y[u * xbuf.shape[1]:(u + 1) * xbuf.shape[1]]
    @pl.loop(0, steps)
    def _(i):
        near_copy(i).wait()
        for u in range(NEAR_STEP):
            p = i * NEAR_STEP + u
            src = src_of(near_pairs[0, p], near_pairs[1, p], place)
            dst = dst_of(near_pairs[0, p], near_pairs[1, p], place)
            dst = jnp.where(p < count, dst, spare)
            dims = (((1,), (1,)), ((), ())) if flip else (((1,), (0,)), ((), ()))
            acc[dst] += lax.dot_general(xbuf[src], nbuf[p], dims, preferred_element_type=jnp.float32)
    o_copies, first = [], 0
    for k, size in enumerate(splits[1]):
        @pl.loop(first, first + size)
        def _(i):
            obuf[i] = acc[i].astype(jnp.bfloat16)
        copy = pltpu.make_async_copy(obuf.at[pl.ds(first, size)], outs[k], osem.at[k])
        copy.start()
        o_copies.append(copy)
        first += size
    for copy in o_copies:
        copy.wait()

def pair_product(flip, vmem_mib, src_of, dst_of, in_sizes, out_sizes, near_pairs, near_count, far_pairs, far_rank, near, proj, back, sources):
    loads, dof = sources[0].shape[-2:]
    smem = pl.BlockSpec(memory_space=pltpu.SMEM)
    hbm = pl.BlockSpec(memory_space=pl.ANY)
    n_dst = sum(out_sizes)
    near_n = near.shape[0]
    return pl.pallas_call(
        functools.partial(pair_kernel, flip, src_of, dst_of, (in_sizes, out_sizes)),
        out_shape=[jax.ShapeDtypeStruct((n, loads, dof), jnp.bfloat16) for n in out_sizes],
        in_specs=[smem] * 4 + [hbm] * (3 + len(sources)),
        out_specs=[hbm] * len(out_sizes),
        scratch_shapes=[
            pltpu.VMEM((sum(size for _, _, size in in_sizes), loads, dof), jnp.bfloat16),
            pltpu.VMEM(near.shape, jnp.bfloat16),
            pltpu.VMEM(proj.shape, jnp.bfloat16),
            pltpu.VMEM(back.shape, jnp.bfloat16),
            pltpu.VMEM((n_dst + 1, loads, dof), jnp.float32),
            pltpu.VMEM((n_dst, loads, dof), jnp.bfloat16),
            pltpu.SemaphoreType.DMA((len(in_sizes),)),
            pltpu.SemaphoreType.DMA((near_n // NEAR_STEP,)),
            pltpu.SemaphoreType.DMA,
            pltpu.SemaphoreType.DMA,
            pltpu.SemaphoreType.DMA((len(out_sizes),)),
        ],
        compiler_params=pltpu.CompilerParams(vmem_limit_bytes=vmem_mib * 2**20),
        cost_estimate=pl.CostEstimate(flops=2 * near_n * loads * dof * dof, bytes_accessed=2 * near.size + 4 * proj.size, transcendentals=0),
    )(near_pairs, near_count, far_pairs, far_rank, near, proj, back, *sources)


SIDE = 4
PER = 8


def col_shift(step, other):
    return [((x + step) % SIDE * 2 + (core ^ other), x * 2 + core) for x in range(SIDE) for core in range(2)]


def plane_shift(first, step):
    pairs = []
    for y in range(SIDE):
        for z in range(SIDE):
            for col in range(2 * SIDE):
                along_y = (col % 2 == 0) == (first == 1)
                far = ((y + step) % SIDE, z) if along_y else (y, (z + step) % SIDE)
                pairs.append(((far[0] * SIDE + far[1]) * 2 * SIDE + col, (y * SIDE + z) * 2 * SIDE + col))
    return pairs


def row_place(r, place):
    piece = (r // PER) % (2 * SIDE)
    return (piece // 2 - place[1] // 2 + SIDE) % SIDE, (piece % 2) ^ (place[1] % 2), r % PER


def src_rows(r, c, place):
    step, other, j = row_place(r, place)
    near_step = jnp.where(place[1] % 2 == 0, SIDE - 1, 1)
    at = jnp.where(step == 0, other, jnp.where(step == 2, 6 + other, jnp.where(step == near_step, 2 + other, 5 - other)))
    return at * PER + j


def dst_rows(r, c, place):
    step, other, j = row_place(r, place)
    mine = (step == jnp.where(place[1] % 2 == 0, 1, SIDE - 1)) | ((step % 2 == 0) & (other == 0))
    at = jnp.where(step == 0, 3, jnp.where(step == 2, 2, jnp.where(mine, other, 1 - other)))
    return (jnp.where(mine, SIDE, 0) + at) * PER + j


def col_place(c, place):
    piece = c // (2 * SIDE * PER)
    dy = (piece // SIDE - place[0] // SIDE + SIDE) % SIDE
    dz = (piece % SIDE - place[0] % SIDE + SIDE) % SIDE
    j = c % PER
    late = j // 4
    return jnp.where(late == 0, dz, dy), jnp.where(late == 0, dy, dz), late, j % 4


def src_cols(r, c, place):
    first, second, late, j = col_place(c, place)
    return (late ^ (place[1] % 2)) * 64 + first * 16 + second * 4 + j


def dst_cols(r, c, place):
    first, second, late, j = col_place(c, place)
    return (late ^ (place[1] % 2)) * 64 + (first + SIDE - 1) % SIDE * 16 + second * 4 + j


def wide(v):
    return v.astype(jnp.float32)


def narrow(v):
    return v.astype(jnp.bfloat16)


def swap(v):
    return lax.ppermute(v, "col", col_shift(0, 1))


def local(
    load_vectors,
    live_panels,
    self_blocks,
    near_pairs,
    near_count,
    near_blocks,
    far_pairs,
    far_rank,
    far_left,
    far_right,
):
    dof = load_vectors.shape[2]
    panel_of = jnp.arange(dof) % (dof // 3)
    masked = load_vectors * (panel_of[None, :] < live_panels[:, None]).astype(jnp.bfloat16)[:, None, :]
    core = lax.axis_index("col") % 2
    twin = swap(masked)
    part = lambda v: lax.dynamic_slice_in_dim(v, core * (PER // 2), PER // 2)
    own = jnp.stack([part(masked), part(twin)])
    plane = lambda v, first, step: lax.ppermute(v, ("row", "col"), plane_shift(first, step))
    chip = [((x - 1 + 2 * core) % SIDE * 2 + core, x * 2 + core) for x in range(SIDE) for core in range(2)]
    x_near = lax.ppermute(masked, "col", chip)
    x_cross = lax.ppermute(twin, "col", chip)
    line = [plane(own, 1, step) for step in (1, 3, 2)]
    x_two = lax.ppermute(x_near, "col", chip)
    x_near, x_cross, line = lax.optimization_barrier((x_near, x_cross, line))
    line = jnp.stack([own, line[0], line[2], line[1]])
    cols = [line] + [plane(line, 0, step) for step in (1, 2, 3)]
    rows = [masked, twin, x_near, x_cross, swap(x_near), swap(x_cross), x_two, swap(x_two)]
    left = jnp.swapaxes(far_left, 1, 2).reshape(-1, dof)
    right = jnp.swapaxes(far_right, 1, 2).reshape(-1, dof)
    lists = (near_pairs.T, near_count, far_pairs.T, far_rank, near_blocks)
    to_cols = pair_product(False, 44, src_rows, dst_cols, [(k, None, n) for k, n in enumerate((8,) * 8)], (16,) * 8, *lists, left, right, rows)
    sums = [jnp.stack([to_cols[k], swap(to_cols[k + SIDE])]) for k in (0, 2)]
    cols[1:], sums = lax.optimization_barrier((cols[1:], sums))
    sums = [sums[0], jnp.stack([to_cols[1], swap(to_cols[5])]), sums[1], jnp.stack([to_cols[3], swap(to_cols[7])])]
    cols += [swap(v[:, 1]) for v in cols]
    sums_in = [plane(sums[step - 1], 0, -step) for step in (1, 2, 3)]
    pieces = [(k, (at, 0) if k < 4 else at, 4) for k in range(8) for at in range(SIDE)]
    to_rows = pair_product(True, 38, src_cols, dst_rows, pieces, (16,) * 4, *lists, right, left, cols)
    row_near = wide(to_rows[2]) + wide(swap(to_rows[0]))
    row_far = wide(to_rows[3]) + wide(swap(to_rows[1]))
    forth = lax.ppermute(narrow(row_far[:PER]), "col", chip)
    cross = lax.ppermute(narrow(row_near[PER:]), "col", chip)
    sums_in = lax.optimization_barrier((row_near, row_far, sums_in))[2]
    split = lambda v: v.reshape((2, SIDE, PER // 2) + masked.shape[1:])
    line_in = [split(v) for v in [sums[3], *sums_in]]
    block = lambda step: sum(wide(v[:, step]) for v in line_in)
    ends = [plane(narrow(block(step)), 1, -step) for step in (1, 2, 3)]
    forth_two = lax.ppermute(narrow(row_near[:PER] + wide(forth)), "col", chip)
    forth_two, ends = lax.optimization_barrier((forth_two, ends))
    end = block(0)
    end_in = wide(swap(narrow(end[1] + sum(wide(v[1]) for v in ends))))
    end_own = end[0] + sum(wide(v[0]) for v in ends)
    own_part = jnp.einsum("cld,ced->cle", masked, self_blocks, preferred_element_type=jnp.float32)
    base = own_part + row_far[PER:] + wide(swap(cross)) + wide(forth_two)
    base, end_in = lax.optimization_barrier((base, end_in))
    total = base + jnp.where(core == 0, jnp.concatenate([end_own, end_in]), jnp.concatenate([end_in, end_own]))
    live_out = (panel_of[None, :] < lax.optimization_barrier(live_panels)[:, None]).astype(jnp.float32)
    return total * live_out[:, None, :]


def solution(mesh):
    spec = P(("row", "col"))
    return jax.shard_map(local, mesh=mesh, in_specs=(spec,) * 10, out_specs=spec, check_vma=False)
```
